32 devices in a mesh: replica: 4 (over y, x), space: 8 (over z, core).
Axes of the slice: x: 2, y: 2, z: 4, core: 2. Of those that a mesh axis runs over, the one named last changes fastest.
Arguments:
- inputs: bfloat16 [4, 64, 512, 256], P('replica', 'space'), may hold values from -6 to 6
- cotangent: bfloat16 [4, 64, 512, 256], P('replica', 'space'), may hold values from -6 to 6
- land_mask: int32 [64, 512], P('space'), may hold values 0 or 1
- weights: float32 [4, 2, 2304, 256], P('replica', None, 'space'), may hold values from -0.125 to 0.125
- momentum: float32 [4, 2, 2304, 256], P('replica', None, 'space'), may hold values from -6 to 6
- step: int32 [1], replicated, may hold values from 0 to 63
Outputs:
- grad_input: bfloat16 [4, 64, 512, 256], P('replica', 'space')
- new_weights: float32 [4, 2, 2304, 256], P('replica', None, 'space')
- new_momentum: float32 [4, 2, 2304, 256], P('replica', None, 'space')
The draws below stay inside these ranges and needn't reach their ends.
All inputs are finite; a program needn't handle non-finite values. No bound on the sum of `land_mask` on one device may be relied on, other than what follows from the above.
Results may differ from the reference program's by a relative error of at most 0.012.
Values may be sent and summed in bfloat16 or wider, within the bound.
A program may use at most 256 MiB of HBM per device.

```python
import math
import jax
import jax.numpy as jnp
from jax import lax

C = 256
COLS = 512
KC = 2304
ROWS = 64
REPLICAS = 4


def touch_ends(drawn, rng, low, high):
    index_at = [jax.random.randint(jax.random.fold_in(rng, axis), (), 0, length) for axis, length in enumerate(drawn.shape)]
    longest = drawn.shape.index(max(drawn.shape))
    neighbour = index_at[:longest] + [(index_at[longest] + 1) % drawn.shape[longest]] + index_at[longest + 1:]
    return drawn.at[tuple(index_at)].set(low).at[tuple(neighbour)].set(high)


def level_of(stream_key, shape, shards, least, top_value):
    factor_of = 1.0
    for dim, shards_of in shards:
        steps = jax.random.uniform(jax.random.fold_in(jax.random.fold_in(stream_key, 6), dim), (shards_of,), jnp.float32, least / len(shards), top_value / len(shards))
        factor_of = factor_of * jnp.repeat(jnp.exp(steps), shape[dim] // shards_of).reshape((-1,) + (1,) * (len(shape) - 1 - dim))
    return factor_of


def gaussian(rng, dims, scale, limit, cuts=(), kind=jnp.bfloat16):
    array = jax.random.normal(rng, dims, jnp.float32) * scale
    if len(cuts) > 0:
        array = level_of(rng, dims, cuts, -0.22, 0.18) * array
    return jnp.clip(array, min=-limit, max=limit).astype(kind)


def setup_inputs(seed: int = 0) -> dict:
    key_of = jax.random.split(jax.random.key(seed), 7)
    return {
        "inputs": gaussian(key_of[0], (REPLICAS, ROWS, COLS, C), 1.0, 6.0, ((0, 4), (1, 8))),
        "cotangent": gaussian(key_of[1], (REPLICAS, ROWS, COLS, C), 1.0, 6.0, ((0, 4), (1, 8))),
        "land_mask": touch_ends((jax.random.randint(key_of[2], (ROWS, COLS), 0, 3) < 2).astype(jnp.int32), jax.random.fold_in(key_of[2], 1), 0, 1),
        "weights": gaussian(key_of[3], (REPLICAS, 2, KC, C), KC ** -0.5, 0.125, ((0, 4), (2, 8)), jnp.float32),
        "momentum": gaussian(key_of[4], (REPLICAS, 2, KC, C), 1.0, 6.0, ((0, 4), (2, 8)), jnp.float32),
        "step": jax.random.randint(key_of[5], (1,), 0, 64).astype(jnp.int32),
    }


def shifted(field, down, right):
    row_count = field.shape[0]
    col_count = field.shape[1]
    padded = jnp.pad(field, ((1, 1), (1, 1), (0, 0)))
    return padded[1 + down:1 + down + row_count, 1 + right:1 + right + col_count]

def kernel_block(kernel, tap_row, tap_col):
    chan_count = kernel.shape[1]
    first_row = (3 * tap_row + tap_col) * chan_count
    return kernel[first_row:first_row + chan_count]

def conv_ahead(field, kernel):
    summed = jnp.zeros(field.shape[:2] + (kernel.shape[1],), jnp.float32)
    for tap_row in range(3):
        for tap_col in range(3):
            summed = summed + jnp.einsum('hwc,cd->hwd', shifted(field, tap_row - 1, tap_col - 1), kernel_block(kernel, tap_row, tap_col))
    return summed

def conv_behind(field, kernel):
    summed = jnp.zeros(field.shape, jnp.float32)
    for tap_row in range(3):
        for tap_col in range(3):
            summed = summed + jnp.einsum('hwd,cd->hwc', shifted(field, 1 - tap_row, 1 - tap_col), kernel_block(kernel, tap_row, tap_col))
    return summed

def kernel_grad(field, upstream):
    blocks = []
    for tap_row in range(3):
        for tap_col in range(3):
            blocks.append(jnp.einsum('hwc,hwd->cd', shifted(field, tap_row - 1, tap_col - 1), upstream))
    return jnp.concatenate(blocks, axis=0)

def silu_slope(preact):
    sigma = jax.nn.sigmoid(preact)
    return sigma * (1.0 + preact * (1.0 - sigma))

def reference(inputs, cotangent, land_mask, weights, momentum, step):
    mask_bf = land_mask.astype(jnp.bfloat16)
    scale = 1.0 / math.sqrt(ROWS * COLS)

    def one_replica(entries):
        field_in, upstream, kernels_f = entries
        masked = upstream * mask_bf[:, :, None]
        kernels = lax.optimization_barrier(kernels_f.astype(jnp.bfloat16)).astype(jnp.float32)
        field_f = field_in.astype(jnp.float32)
        masked_f = masked.astype(jnp.float32)
        preact = conv_ahead(field_f, kernels[0])
        hidden = lax.optimization_barrier(jax.nn.silu(preact).astype(jnp.bfloat16)).astype(jnp.float32)
        back_hidden = conv_behind(masked_f, kernels[1])
        back_pre = lax.optimization_barrier((back_hidden * silu_slope(preact)).astype(jnp.bfloat16)).astype(jnp.float32)
        grad_in = (conv_behind(back_pre, kernels[0]) + masked_f).astype(jnp.bfloat16)
        grads = jnp.stack([kernel_grad(field_f, back_pre), kernel_grad(hidden, masked_f)]) * scale
        return (grad_in, grads)
    grad_input, grads = lax.map(one_replica, (inputs, cotangent, weights))
    moment = 0.9 * momentum + grads
    updated = weights - 0.01 * moment
    levels = REPLICAS.bit_length() - 1
    distance = jnp.left_shift(jnp.int32(1), step[0] % levels)
    new_weights = 0.5 * (updated + jnp.roll(updated, distance, axis=0))
    new_momentum = 0.5 * (moment + jnp.roll(moment, distance, axis=0))
    return (grad_input, new_weights, new_momentum)
```

```python
from functools import partial
import math

import jax
import jax.numpy as jnp
from jax import lax
from jax.experimental import pallas as pl
from jax.experimental.pallas import tpu as pltpu
from jax.sharding import PartitionSpec as P

F32 = jnp.float32
BF16 = jnp.bfloat16
MESH = pl.DeviceIdType.MESH


def block_kernel(
    n, reps, levels, scale,
    coef, x_hbm, cot_hbm, mask_ref, w_ref, mom_ref,
    gi_hbm, nw_ref, nm_ref,
    xs, ms, ps, x_t, h_t, slope, cot, gi, kf, k_t, wb, mb, gb, sib, pair, far, gk, gw, gm, gg,
    loc_sem, halo_send, halo_recv, ag_send, ag_recv, agf_send, agf_recv,
    rs1_send, rs1_recv, rs2_send, rs2_recv, go_send, go_recv,
):
    rows, cols, chans = x_hbm.shape
    ext = rows + 2
    nz = n // 2
    sh = w_ref.shape[1]
    taps = 9
    q = lax.axis_index("replica")
    s = lax.axis_index("space")
    z = s // 2
    c = s % 2
    other = s + 1 - 2 * c

    def span(r, count=1):
        return pl.ds(pl.multiple_of(r * cols, cols), count * cols)

    def shard_rows(i):
        return pl.ds(pl.multiple_of(i * sh, 16), sh)

    def send(src, dst, ssem, rsem, rep, spc):
        return pltpu.make_async_remote_copy(
            src_ref=src, dst_ref=dst, send_sem=ssem, recv_sem=rsem,
            device_id=(rep, spc), device_id_type=MESH)

    started = []

    x_in = [pltpu.make_async_copy(x_hbm.at[r], xs.at[1, pl.ds((r + 1) * cols, cols)], loc_sem.at[r])
            for r in range(rows)]
    c_in = [pltpu.make_async_copy(cot_hbm.at[r], cot.at[pl.ds(r * cols, cols)], loc_sem.at[rows + r])
            for r in range(rows)]
    order = [0, rows - 1] + list(range(1, rows - 1))
    for r in order:
        x_in[r].start()
    for r in order:
        c_in[r].start()

    wb[...] = w_ref[...].astype(BF16)
    for k in range(2):
        kf[k, shard_rows(s), :] = w_ref[k].astype(BF16)

    barrier = pltpu.get_barrier_semaphore()
    for o in range(1, n):
        pl.semaphore_signal(barrier, inc=1, device_id=(q, (s + o) % n), device_id_type=MESH)
    for o in range(1, reps):
        pl.semaphore_signal(barrier, inc=1, device_id=((q + o) % reps, s), device_id_type=MESH)
    pl.semaphore_wait(barrier, n - 1 + reps - 1)

    def gather_start(k):
        out = []
        for o in range(1, nz):
            cp = send(kf.at[k, shard_rows(s)], kf.at[k, shard_rows(s)],
                      ag_send.at[k, o], ag_recv.at[k, o], q, ((z + o) % nz) * 2 + c)
            cp.start()
            out.append(cp)
        cp = send(kf.at[k, shard_rows(s)], kf.at[k, shard_rows(s)],
                  agf_send.at[k, 0], agf_recv.at[k, 0], q, other)
        cp.start()
        started.extend(out + [cp])
        return out, [cp]

    def gather_pass(k, far_copies, sib_copies):
        for o in range(1, nz):
            far_copies[o - 1].wait_recv()
            origin = ((z + nz - o) % nz) * 2 + c
            cp = send(kf.at[k, shard_rows(origin)], kf.at[k, shard_rows(origin)],
                      agf_send.at[k, o], agf_recv.at[k, o], q, other)
            cp.start()
            sib_copies.append(cp)
            started.append(cp)

    def gather_finish(sib_copies):
        for cp in sib_copies:
            cp.wait_recv()

    def halo(f, buf, go):
        lower = send(buf.at[1, span(1)], buf.at[1, span(ext - 1)],
                     halo_send.at[f, 0], halo_recv.at[f, 0], q, (s + n - 1) % n)
        upper = send(buf.at[1, span(rows)], buf.at[1, span(0)],
                     halo_send.at[f, 1], halo_recv.at[f, 1], q, (s + 1) % n)
        if go:
            @pl.when(s > 0)
            def _():
                lower.start()

            @pl.when(s < n - 1)
            def _():
                upper.start()
        else:
            @pl.when(s < n - 1)
            def _():
                lower.wait_recv()

            @pl.when(s > 0)
            def _():
                upper.wait_recv()

            @pl.when(s > 0)
            def _():
                lower.wait_send()

            @pl.when(s < n - 1)
            def _():
                upper.wait_send()

            @pl.when(s == 0)
            def _():
                buf[1, span(0), :] = jnp.zeros((cols, chans), BF16)

            @pl.when(s == n - 1)
            def _():
                buf[1, span(ext - 1), :] = jnp.zeros((cols, chans), BF16)

    def sides(buf, r, v):
        col = lax.broadcasted_iota(jnp.int32, (cols, chans), 0)
        buf[0, span(r), :] = jnp.where(col == 0, 0.0, pltpu.roll(v, 1, 0)).astype(BF16)
        buf[2, span(r), :] = jnp.where(col == cols - 1, 0.0, pltpu.roll(v, cols - 1, 0)).astype(BF16)

    far0, sib0 = gather_start(0)

    for r in order[:2]:
        x_in[r].wait()
    halo(0, xs, True)
    mask_t = jnp.transpose(mask_ref[...].astype(F32))

    def mask_row(r):
        c_in[r].wait()
        v = cot[pl.ds(r * cols, cols), :].astype(F32) * mask_t[:, r:r + 1]
        ms[1, pl.ds((r + 1) * cols, cols), :] = v.astype(BF16)
        sides(ms, r + 1, v)

    for r in order[:2]:
        mask_row(r)
    halo(1, ms, True)
    for r in order[2:]:
        x_in[r].wait()

    mb[...] = mom_ref[...].astype(BF16)
    for level in range(levels):
        to = (q + (1 << level)) % reps
        for j, (src, dst) in enumerate(((wb, gw), (mb, gm))):
            cp = send(src, dst.at[level], go_send.at[j, level], go_recv.at[j, level], to, s)
            cp.start()
            started.append(cp)
    early = started[-2 * levels:]

    for r in order[2:]:
        mask_row(r)

    def prep_x(r):
        v = xs[1, span(r), :]
        x_t[:, span(r)] = jnp.transpose(v)
        sides(xs, r, v.astype(F32))

    @pl.loop(1, rows + 1)
    def _(r):
        prep_x(r)

    halo(0, xs, False)
    prep_x(0)
    prep_x(ext - 1)
    halo(1, ms, False)
    sides(ms, 0, ms[1, span(0), :].astype(F32))
    sides(ms, ext - 1, ms[1, span(ext - 1), :].astype(F32))

    gather_pass(0, far0, sib0)
    far1, sib1 = gather_start(1)
    gather_finish(sib0)

    def conv(buf, ker, h, ahead):
        parts = []
        for i in range(3):
            for j in range(3):
                a, b = (i, j) if ahead else (2 - i, 2 - j)
                parts.append(buf[b, span(h + a), :])
        return jnp.dot(jnp.concatenate(parts, axis=1), ker[...], preferred_element_type=F32)

    def turn(k):
        @pl.loop(0, taps)
        def _(t):
            at = pl.ds(pl.multiple_of(t * chans, chans), chans)
            k_t[k, at, :] = jnp.transpose(kf[k, at, :])

    @pl.loop(0, rows)
    def _(h):
        pre = conv(xs, kf.at[0], h, True)
        sig = 1.0 / (1.0 + jnp.exp(-pre))
        slope[span(h), :] = sig * (1.0 + pre * (1.0 - sig))
        h_t[:, span(h)] = jnp.transpose((pre * sig).astype(BF16))

    def grads(k, lhs_of, rhs_of):
        @pl.loop(0, taps)
        def _(t):
            i = t // 3
            j = t % 3
            g = jnp.dot(lhs_of(i), rhs_of(i, j), preferred_element_type=F32)
            gb[k, pl.ds(pl.multiple_of(t * chans, chans), chans), :] = (g * scale).astype(BF16)

    def share_start(k):
        out = []
        for y in range(nz):
            cp = send(gb.at[k, shard_rows(2 * y + 1 - c)], sib.at[k, y],
                      rs1_send.at[k, y], rs1_recv.at[k, y], q, other)
            cp.start()
            out.append(cp)
        started.extend(out)
        return out

    def share_pass(k, copies):
        out = []
        for cp in copies:
            cp.wait_recv()
        for o in list(range(1, nz)) + [0]:
            y = (z + o) % nz
            both = gb[k, shard_rows(2 * y + c), :].astype(F32) + sib[k, y].astype(F32)
            pair[k, o] = both.astype(BF16)
            if o:
                cp = send(pair.at[k, o], far.at[k, o], rs2_send.at[k, o], rs2_recv.at[k, o],
                          q, y * 2 + c)
                cp.start()
                out.append(cp)
        started.extend(out)
        return out

    def share_finish(k, copies):
        total = pair[k, 0].astype(F32)
        for o in range(1, nz):
            copies[o - 1].wait_recv()
            total = total + far[k, o].astype(F32)
        gk[k] = total.astype(BF16)
        nm_ref[k] = total
        out = []
        for level in range(levels):
            cp = send(gk.at[k], gg.at[k, level], go_send.at[2 + k, level], go_recv.at[2 + k, level],
                      (q + (1 << level)) % reps, s)
            cp.start()
            out.append(cp)
        started.extend(out)
        return out

    def settle(k, copies):
        for cp in copies:
            cp.wait_recv()
        g_in = jnp.zeros((sh, chans), F32)
        m_in = jnp.zeros((sh, chans), F32)
        w_in = jnp.zeros((sh, chans), F32)
        for level in range(levels):
            g_in = g_in + coef[level] * gg[k, level].astype(F32)
            m_in = m_in + coef[level] * gm[level, k].astype(F32)
            w_in = w_in + coef[level] * gw[level, k].astype(F32)
        mixed = 0.5 * (0.9 * (mom_ref[k] + m_in) + nm_ref[k] + g_in)
        nm_ref[k] = mixed
        nw_ref[k] = 0.5 * (w_ref[k] + w_in) - 0.01 * mixed

    grads(1, lambda i: h_t[...], lambda i, j: ms[2 - j, span(2 - i, rows), :])
    share1 = share_start(1)
    gather_pass(1, far1, sib1)
    turn(0)
    gather_finish(sib1)
    turn(1)

    def back(h):
        v = conv(ms, k_t.at[1], h, False) * slope[span(h), :]
        ps[1, span(h + 1), :] = v.astype(BF16)
        sides(ps, h + 1, v)

    @pl.loop(0, 2)
    def _(t):
        back(t * (rows - 1))

    halo(2, ps, True)
    parts1 = share_pass(1, share1)

    @pl.loop(1, rows - 1)
    def _(h):
        back(h)

    grads(0, lambda i: x_t[:, span(i, rows)], lambda i, j: ps[2 - j, span(1, rows), :])
    share0 = share_start(0)

    def out_row(h):
        v = conv(ps, k_t.at[0], h, False) + ms[1, span(h + 1), :].astype(F32)
        gi[span(h), :] = v.astype(BF16)

    halo(2, ps, False)
    sides(ps, 0, ps[1, span(0), :].astype(F32))
    sides(ps, ext - 1, ps[1, span(ext - 1), :].astype(F32))
    parts0 = share_pass(0, share0)
    half = rows // 2

    @pl.loop(0, half)
    def _(h):
        out_row(h)

    last1 = share_finish(1, parts1)

    @pl.loop(half, rows)
    def _(h):
        out_row(h)

    stores = [pltpu.make_async_copy(gi.at[pl.ds(r * cols, cols)], gi_hbm.at[r], loc_sem.at[r])
              for r in range(rows)]
    for cp in stores:
        cp.start()
    for cp in early:
        cp.wait_recv()
    last0 = share_finish(0, parts0)
    settle(1, last1)
    settle(0, last0)
    for cp in stores:
        cp.wait()
    for cp in started:
        cp.wait_send()


def shards(inputs, cotangent, land_mask, weights, momentum, step):
    n = lax.axis_size("space")
    reps = lax.axis_size("replica")
    levels = reps.bit_length() - 1
    rows, cols, chans = inputs.shape[1:]
    sh = weights.shape[2]
    kc = sh * n
    ext = rows + 2
    nz = n // 2
    scale = 1.0 / math.sqrt(rows * n * cols)
    coef = (step[0] % levels == jnp.arange(levels)).astype(F32)
    vm = pltpu.VMEM
    sem = pltpu.SemaphoreType.DMA
    flops = 5 * 2 * rows * cols * kc * chans
    any_space = pl.BlockSpec(memory_space=pl.ANY)
    in_vmem = pl.BlockSpec(memory_space=pltpu.VMEM)
    gi, nw, nm = pl.pallas_call(
        partial(block_kernel, n, reps, levels, scale),
        out_shape=(
            jax.ShapeDtypeStruct((rows, cols, chans), BF16),
            jax.ShapeDtypeStruct((2, sh, chans), F32),
            jax.ShapeDtypeStruct((2, sh, chans), F32),
        ),
        in_specs=[pl.BlockSpec(memory_space=pltpu.SMEM), any_space, any_space,
                  in_vmem, in_vmem, in_vmem],
        out_specs=(any_space, in_vmem, in_vmem),
        scratch_shapes=[
            vm((3, ext * cols, chans), BF16),
            vm((3, ext * cols, chans), BF16),
            vm((3, ext * cols, chans), BF16),
            vm((chans, ext * cols), BF16),
            vm((chans, rows * cols), BF16),
            vm((rows * cols, chans), F32),
            vm((rows * cols, chans), BF16),
            vm((rows * cols, chans), BF16),
            vm((2, kc, chans), BF16),
            vm((2, kc, chans), BF16),
            vm((2, sh, chans), BF16),
            vm((2, sh, chans), BF16),
            vm((2, kc, chans), BF16),
            vm((2, nz, sh, chans), BF16),
            vm((2, nz, sh, chans), BF16),
            vm((2, nz, sh, chans), BF16),
            vm((2, sh, chans), BF16),
            vm((levels, 2, sh, chans), BF16),
            vm((levels, 2, sh, chans), BF16),
            vm((2, levels, sh, chans), BF16),
            sem((2 * rows,)),
            sem((3, 2)), sem((3, 2)),
            sem((2, nz)), sem((2, nz)), sem((2, nz)), sem((2, nz)),
            sem((2, nz)), sem((2, nz)), sem((2, nz)), sem((2, nz)),
            sem((4, levels)), sem((4, levels)),
        ],
        compiler_params=pltpu.CompilerParams(
            collective_id=0, has_side_effects=True, vmem_limit_bytes=60 * 1024 * 1024),
        cost_estimate=pl.CostEstimate(flops=flops, bytes_accessed=12 << 20, transcendentals=0),
    )(coef, inputs[0], cotangent[0], land_mask, weights[0], momentum[0])
    return gi[None], nw[None], nm[None]


def solution(mesh):
    in_specs = (
        P("replica", "space", None, None),
        P("replica", "space", None, None),
        P("space", None),
        P("replica", None, "space", None),
        P("replica", None, "space", None),
        P(),
    )
    out_specs = (
        P("replica", "space", None, None),
        P("replica", None, "space", None),
        P("replica", None, "space", None),
    )
    return jax.shard_map(shards, mesh=mesh, in_specs=in_specs, out_specs=out_specs, check_vma=False)
```

```python
from functools import partial
import math

import jax
import jax.numpy as jnp
from jax import lax
from jax.experimental import pallas as pl
from jax.experimental.pallas import tpu as pltpu
from jax.sharding import PartitionSpec as P

F32 = jnp.float32
BF16 = jnp.bfloat16
MESH = pl.DeviceIdType.MESH


def block_kernel(
    n, reps, levels, scale,
    coef, x_hbm, cot_hbm, mask_ref, w_ref, mom_ref,
    gi_hbm, nw_ref, nm_ref,
    xs, ms, ps, x_t, m_t, hid, slope, cot, kf, k_t, wb, mb, gb, sib, pair, far, gk, gw, gm, gg,
    loc_sem, halo_send, halo_recv, ag_send, ag_recv, agf_send, agf_recv,
    rs1_send, rs1_recv, rs2_send, rs2_recv, go_send, go_recv,
):
    rows, cols, chans = x_hbm.shape
    ext = rows + 2
    nz = n // 2
    sh = w_ref.shape[1]
    taps = 9
    q = lax.axis_index("replica")
    s = lax.axis_index("space")
    z = s // 2
    c = s % 2
    other = s + 1 - 2 * c

    def span(r, count=1):
        return pl.ds(pl.multiple_of(r * cols, cols), count * cols)

    def shard_rows(i):
        return pl.ds(pl.multiple_of(i * sh, 16), sh)

    def send(src, dst, ssem, rsem, rep, spc):
        return pltpu.make_async_remote_copy(
            src_ref=src, dst_ref=dst, send_sem=ssem, recv_sem=rsem,
            device_id=(rep, spc), device_id_type=MESH)

    started = []

    x_in = [pltpu.make_async_copy(x_hbm.at[r], xs.at[1, pl.ds((r + 1) * cols, cols)], loc_sem.at[r])
            for r in range(rows)]
    c_in = [pltpu.make_async_copy(cot_hbm.at[r], cot.at[pl.ds(r * cols, cols)], loc_sem.at[rows + r])
            for r in range(rows)]
    order = [0, rows - 1] + list(range(1, rows - 1))
    for r in order:
        x_in[r].start()
    for r in order:
        c_in[r].start()

    wb[...] = w_ref[...].astype(BF16)
    for k in range(2):
        kf[k, shard_rows(s), :] = w_ref[k].astype(BF16)

    barrier = pltpu.get_barrier_semaphore()
    for o in range(1, n):
        pl.semaphore_signal(barrier, inc=1, device_id=(q, (s + o) % n), device_id_type=MESH)
    for o in range(1, reps):
        pl.semaphore_signal(barrier, inc=1, device_id=((q + o) % reps, s), device_id_type=MESH)
    pl.semaphore_wait(barrier, n - 1 + reps - 1)

    def gather_start(k):
        out = []
        for o in range(1, nz):
            cp = send(kf.at[k, shard_rows(s)], kf.at[k, shard_rows(s)],
                      ag_send.at[k, o], ag_recv.at[k, o], q, ((z + o) % nz) * 2 + c)
            cp.start()
            out.append(cp)
        cp = send(kf.at[k, shard_rows(s)], kf.at[k, shard_rows(s)],
                  agf_send.at[k, 0], agf_recv.at[k, 0], q, other)
        cp.start()
        started.extend(out + [cp])
        return out, [cp]

    def gather_pass(k, far_copies, sib_copies):
        for o in range(1, nz):
            far_copies[o - 1].wait_recv()
            origin = ((z + nz - o) % nz) * 2 + c
            cp = send(kf.at[k, shard_rows(origin)], kf.at[k, shard_rows(origin)],
                      agf_send.at[k, o], agf_recv.at[k, o], q, other)
            cp.start()
            sib_copies.append(cp)
            started.append(cp)

    def gather_finish(sib_copies):
        for cp in sib_copies:
            cp.wait_recv()

    def halo(f, buf, go):
        lower = send(buf.at[1, span(1)], buf.at[1, span(ext - 1)],
                     halo_send.at[f, 0], halo_recv.at[f, 0], q, (s + n - 1) % n)
        upper = send(buf.at[1, span(rows)], buf.at[1, span(0)],
                     halo_send.at[f, 1], halo_recv.at[f, 1], q, (s + 1) % n)
        if go:
            @pl.when(s > 0)
            def _():
                lower.start()

            @pl.when(s < n - 1)
            def _():
                upper.start()
        else:
            @pl.when(s < n - 1)
            def _():
                lower.wait_recv()

            @pl.when(s > 0)
            def _():
                upper.wait_recv()

            @pl.when(s > 0)
            def _():
                lower.wait_send()

            @pl.when(s < n - 1)
            def _():
                upper.wait_send()

            @pl.when(s == 0)
            def _():
                buf[1, span(0), :] = jnp.zeros((cols, chans), BF16)

            @pl.when(s == n - 1)
            def _():
                buf[1, span(ext - 1), :] = jnp.zeros((cols, chans), BF16)

    def sides(buf, r, v):
        col = lax.broadcasted_iota(jnp.int32, (cols, chans), 0)
        left = jnp.where(col == 0, 0.0, pltpu.roll(v, 1, 0)).astype(BF16)
        right = jnp.where(col == cols - 1, 0.0, pltpu.roll(v, cols - 1, 0)).astype(BF16)
        buf[0, span(r), :] = left
        buf[2, span(r), :] = right
        return left, right

    far0, sib0 = gather_start(0)

    for r in order[:2]:
        x_in[r].wait()
    halo(0, xs, True)
    mask_t = jnp.transpose(mask_ref[...].astype(F32))

    def mask_row(r):
        c_in[r].wait()
        v = cot[pl.ds(r * cols, cols), :].astype(F32) * mask_t[:, r:r + 1]
        ms[1, pl.ds((r + 1) * cols, cols), :] = v.astype(BF16)

    for r in order[:2]:
        mask_row(r)
    halo(1, ms, True)
    for r in order[2:]:
        x_in[r].wait()

    mb[...] = mom_ref[...].astype(BF16)
    for level in range(levels):
        to = (q + (1 << level)) % reps
        for j, (src, dst) in enumerate(((wb, gw), (mb, gm))):
            cp = send(src, dst.at[level], go_send.at[j, level], go_recv.at[j, level], to, s)
            cp.start()
            started.append(cp)
    early = started[-2 * levels:]

    for r in order[2:]:
        mask_row(r)

    def prep_x(r, offsets):
        v = xs[1, span(r), :]
        flat = jnp.transpose(v)
        for i in offsets:
            x_t[pl.ds(i * chans, chans), span(r - i)] = flat
        sides(xs, r, v.astype(F32))

    def prep_m(r):
        v = ms[1, span(r), :]
        left, right = sides(ms, r, v.astype(F32))
        for i, part in enumerate((left, v, right)):
            m_t[pl.ds(i * chans, chans), span(r)] = jnp.transpose(part)

    @pl.loop(2, rows)
    def _(r):
        prep_x(r, (0, 1, 2))

    prep_x(1, (0, 1))
    prep_x(rows, (1, 2))
    halo(0, xs, False)
    prep_x(0, (0,))
    prep_x(ext - 1, (2,))

    gather_pass(0, far0, sib0)
    far1, sib1 = gather_start(1)
    halo(1, ms, False)

    @pl.loop(0, ext)
    def _(r):
        prep_m(r)

    gather_finish(sib0)

    def conv(buf, ker, h, ahead):
        parts = []
        for i in range(3):
            for j in range(3):
                a, b = (i, j) if ahead else (2 - i, 2 - j)
                parts.append(buf[b, span(h + a, 2), :])
        return jnp.dot(jnp.concatenate(parts, axis=1), ker[...], preferred_element_type=F32)

    def turn(k):
        @pl.loop(0, taps)
        def _(t):
            at = pl.ds(pl.multiple_of(t * chans, chans), chans)
            k_t[k, at, :] = jnp.transpose(kf[k, at, :])

    @pl.loop(0, rows, step=2, unroll=2)
    def _(h):
        pre = conv(xs, kf.at[0], h, True)
        sig = 1.0 / (1.0 + jnp.exp(-pre))
        slope[span(h, 2), :] = sig * (1.0 + pre * (1.0 - sig))
        hid[span(h, 2), :] = (pre * sig).astype(BF16)

    def put_grad(k, tap, g):
        gb[k, pl.ds(pl.multiple_of(tap * chans, chans), chans), :] = (g * scale).astype(BF16)

    def share_start(k):
        out = []
        for y in range(nz):
            cp = send(gb.at[k, shard_rows(2 * y + 1 - c)], sib.at[k, y],
                      rs1_send.at[k, y], rs1_recv.at[k, y], q, other)
            cp.start()
            out.append(cp)
        started.extend(out)
        return out

    def share_pass(k, copies):
        out = []
        for cp in copies:
            cp.wait_recv()
        for o in list(range(1, nz)) + [0]:
            y = (z + o) % nz
            both = gb[k, shard_rows(2 * y + c), :].astype(F32) + sib[k, y].astype(F32)
            pair[k, o] = both.astype(BF16)
            if o:
                cp = send(pair.at[k, o], far.at[k, o], rs2_send.at[k, o], rs2_recv.at[k, o],
                          q, y * 2 + c)
                cp.start()
                out.append(cp)
        started.extend(out)
        return out

    def share_finish(k, copies):
        total = pair[k, 0].astype(F32)
        for o in range(1, nz):
            copies[o - 1].wait_recv()
            total = total + far[k, o].astype(F32)
        gk[k] = total.astype(BF16)
        nm_ref[k] = total
        out = []
        for level in range(levels):
            cp = send(gk.at[k], gg.at[k, level], go_send.at[2 + k, level], go_recv.at[2 + k, level],
                      (q + (1 << level)) % reps, s)
            cp.start()
            out.append(cp)
        started.extend(out)
        return out

    def settle(k, copies):
        for cp in copies:
            cp.wait_recv()
        g_in = jnp.zeros((sh, chans), F32)
        m_in = jnp.zeros((sh, chans), F32)
        w_in = jnp.zeros((sh, chans), F32)
        for level in range(levels):
            g_in = g_in + coef[level] * gg[k, level].astype(F32)
            m_in = m_in + coef[level] * gm[level, k].astype(F32)
            w_in = w_in + coef[level] * gw[level, k].astype(F32)
        mixed = 0.5 * (0.9 * (mom_ref[k] + m_in) + nm_ref[k] + g_in)
        nm_ref[k] = mixed
        nw_ref[k] = 0.5 * (w_ref[k] + w_in) - 0.01 * mixed

    @pl.loop(0, 3)
    def _(i):
        g = jnp.dot(m_t[:, span(2 - i, rows)], hid[...], preferred_element_type=F32)
        for j in range(3):
            put_grad(1, 3 * i + j, jnp.transpose(g[(2 - j) * chans:(3 - j) * chans]))

    share1 = share_start(1)
    gather_pass(1, far1, sib1)
    turn(0)
    gather_finish(sib1)
    turn(1)

    def back(h):
        v = conv(ms, k_t.at[1], h, False) * slope[span(h, 2), :]
        ps[1, span(h + 1, 2), :] = v.astype(BF16)
        sides(ps, h + 1, v[:cols])
        sides(ps, h + 2, v[cols:])

    @pl.loop(0, 2, unroll=2)
    def _(t):
        back(t * (rows - 2))

    halo(2, ps, True)
    parts1 = share_pass(1, share1)

    @pl.loop(2, rows - 2, step=2, unroll=2)
    def _(h):
        back(h)

    @pl.loop(0, 3)
    def _(j):
        g = jnp.dot(x_t[...], ps[2 - j, span(1, rows), :], preferred_element_type=F32)
        for i in range(3):
            put_grad(0, 3 * i + j, g[i * chans:(i + 1) * chans])

    share0 = share_start(0)

    def out_row(h):
        v = conv(ps, k_t.at[0], h, False) + ms[1, span(h + 1, 2), :].astype(F32)
        cot[span(h, 2), :] = v.astype(BF16)

    halo(2, ps, False)
    sides(ps, 0, ps[1, span(0), :].astype(F32))
    sides(ps, ext - 1, ps[1, span(ext - 1), :].astype(F32))
    parts0 = share_pass(0, share0)
    half = rows // 2

    @pl.loop(0, half, step=2, unroll=2)
    def _(h):
        out_row(h)

    last1 = share_finish(1, parts1)

    @pl.loop(half, rows, step=2, unroll=2)
    def _(h):
        out_row(h)

    stores = [pltpu.make_async_copy(cot.at[pl.ds(r * cols, cols)], gi_hbm.at[r], loc_sem.at[r])
              for r in range(rows)]
    for cp in stores:
        cp.start()
    for cp in early:
        cp.wait_recv()
    last0 = share_finish(0, parts0)
    settle(1, last1)
    settle(0, last0)
    for cp in stores:
        cp.wait()
    for cp in started:
        cp.wait_send()


def copy_kernel(gi, nw, nm, gi_out, nw_out, nm_out, done):
    rows = gi.shape[0]
    moves = [(gi.at[r], gi_out.at[r]) for r in range(rows)]
    moves += [(nw.at[k], nw_out.at[k]) for k in range(2)] + [(nm.at[k], nm_out.at[k]) for k in range(2)]
    copies = [pltpu.make_async_copy(a, b, done.at[i]) for i, (a, b) in enumerate(moves)]
    for cp in copies:
        cp.start()
    for cp in copies:
        cp.wait()


def shards(inputs, cotangent, land_mask, weights, momentum, step):
    n = lax.axis_size("space")
    reps = lax.axis_size("replica")
    levels = reps.bit_length() - 1
    rows, cols, chans = inputs.shape[1:]
    sh = weights.shape[2]
    kc = sh * n
    ext = rows + 2
    nz = n // 2
    scale = 1.0 / math.sqrt(rows * n * cols)
    coef = (step[0] % levels == jnp.arange(levels)).astype(F32)
    vm = pltpu.VMEM
    sem = pltpu.SemaphoreType.DMA
    flops = 5 * 2 * rows * cols * kc * chans
    any_space = pl.BlockSpec(memory_space=pl.ANY)
    in_vmem = pl.BlockSpec(memory_space=pltpu.VMEM)
    gi, nw, nm = pl.pallas_call(
        partial(block_kernel, n, reps, levels, scale),
        out_shape=(
            jax.ShapeDtypeStruct((rows, cols, chans), BF16),
            jax.ShapeDtypeStruct((2, sh, chans), F32),
            jax.ShapeDtypeStruct((2, sh, chans), F32),
        ),
        in_specs=[pl.BlockSpec(memory_space=pltpu.SMEM), any_space, any_space,
                  in_vmem, in_vmem, in_vmem],
        out_specs=(any_space, in_vmem, in_vmem),
        scratch_shapes=[
            vm((3, ext * cols, chans), BF16),
            vm((3, ext * cols, chans), BF16),
            vm((3, ext * cols, chans), BF16),
            vm((3 * chans, rows * cols), BF16),
            vm((3 * chans, ext * cols), BF16),
            vm((rows * cols, chans), BF16),
            vm((rows * cols, chans), F32),
            vm((rows * cols, chans), BF16),
            vm((2, kc, chans), BF16),
            vm((2, kc, chans), BF16),
            vm((2, sh, chans), BF16),
            vm((2, sh, chans), BF16),
            vm((2, kc, chans), BF16),
            vm((2, nz, sh, chans), BF16),
            vm((2, nz, sh, chans), BF16),
            vm((2, nz, sh, chans), BF16),
            vm((2, sh, chans), BF16),
            vm((levels, 2, sh, chans), BF16),
            vm((levels, 2, sh, chans), BF16),
            vm((2, levels, sh, chans), BF16),
            sem((2 * rows,)),
            sem((3, 2)), sem((3, 2)),
            sem((2, nz)), sem((2, nz)), sem((2, nz)), sem((2, nz)),
            sem((2, nz)), sem((2, nz)), sem((2, nz)), sem((2, nz)),
            sem((4, levels)), sem((4, levels)),
        ],
        compiler_params=pltpu.CompilerParams(
            collective_id=0, has_side_effects=True, vmem_limit_bytes=63 * 1024 * 1024),
        cost_estimate=pl.CostEstimate(flops=flops, bytes_accessed=12 << 20, transcendentals=0),
    )(coef, inputs[0], cotangent[0], land_mask, weights[0], momentum[0])
    gi, nw, nm = pl.pallas_call(
        copy_kernel,
        out_shape=tuple(jax.ShapeDtypeStruct(v.shape, v.dtype) for v in (gi, nw, nm)),
        in_specs=[any_space] * 3,
        out_specs=(any_space,) * 3,
        scratch_shapes=[sem((rows + 4,))],
    )(gi, nw, nm)
    return gi[None], nw[None], nm[None]


def solution(mesh):
    in_specs = (
        P("replica", "space", None, None),
        P("replica", "space", None, None),
        P("space", None),
        P("replica", None, "space", None),
        P("replica", None, "space", None),
        P(),
    )
    out_specs = (
        P("replica", "space", None, None),
        P("replica", None, "space", None),
        P("replica", None, "space", None),
    )
    return jax.shard_map(shards, mesh=mesh, in_specs=in_specs, out_specs=out_specs, check_vma=False)
```

```python
from functools import partial
import math

import jax
import jax.numpy as jnp
from jax import lax
from jax.experimental import pallas as pl
from jax.experimental.pallas import tpu as pltpu
from jax.sharding import PartitionSpec as P

F32 = jnp.float32
BF16 = jnp.bfloat16
MESH = pl.DeviceIdType.MESH


def block_kernel(
    n, reps, levels, scale,
    coef, x_hbm, cot_hbm, mask_ref, w_ref, mom_ref,
    gi_hbm, nw_ref, nm_ref,
    xs, ms, ps, x_t, m_t, hid, slope, cot, kf, k_t, wb, mb, gb, sib, pair, far, gk, gw, gm, gg,
    loc_sem, halo_send, halo_recv, ag_send, ag_recv, agf_send, agf_recv,
    rs1_send, rs1_recv, rs2_send, rs2_recv, go_send, go_recv,
):
    rows, cols, chans = x_hbm.shape
    ext = rows + 2
    nz = n // 2
    sh = w_ref.shape[1]
    taps = 9
    q = lax.axis_index("replica")
    s = lax.axis_index("space")
    z = s // 2
    c = s % 2
    other = s + 1 - 2 * c

    def span(r, count=1):
        return pl.ds(pl.multiple_of(r * cols, cols), count * cols)

    def shard_rows(i):
        return pl.ds(pl.multiple_of(i * sh, 16), sh)

    def send(src, dst, ssem, rsem, rep, spc):
        return pltpu.make_async_remote_copy(
            src_ref=src, dst_ref=dst, send_sem=ssem, recv_sem=rsem,
            device_id=(rep, spc), device_id_type=MESH)

    started = []

    x_in = [pltpu.make_async_copy(x_hbm.at[r], xs.at[1, pl.ds((r + 1) * cols, cols)], loc_sem.at[r])
            for r in range(rows)]
    c_in = [pltpu.make_async_copy(cot_hbm.at[r], cot.at[pl.ds(r * cols, cols)], loc_sem.at[rows + r])
            for r in range(rows)]
    order = [0, rows - 1] + list(range(1, rows - 1))
    for r in order:
        x_in[r].start()
    for r in order:
        c_in[r].start()

    wb[...] = w_ref[...].astype(BF16)
    for k in range(2):
        kf[k, shard_rows(s), :] = w_ref[k].astype(BF16)

    barrier = pltpu.get_barrier_semaphore()
    for o in range(1, n):
        pl.semaphore_signal(barrier, inc=1, device_id=(q, (s + o) % n), device_id_type=MESH)
    for o in range(1, reps):
        pl.semaphore_signal(barrier, inc=1, device_id=((q + o) % reps, s), device_id_type=MESH)
    pl.semaphore_wait(barrier, n - 1 + reps - 1)

    def shard_send(k, chip, core, ssem, rsem, spc):
        at = shard_rows(2 * chip + core)
        return send(kf.at[k, at], kf.at[k, at], ssem, rsem, q, spc)

    def may_send(d, hop):
        if d == 0:
            return (z + 1 >= hop) & (z + 1 < nz)
        return (z + hop <= nz) & (z >= 1)

    def has_come(d, hop):
        return z >= hop if d == 0 else z + hop < nz

    def hop_copy(k, d, hop):
        chip = z + 1 - hop if d == 0 else z - 1 + hop
        to = s + 2 if d == 0 else s - 2
        return shard_send(k, chip, c, ag_send.at[k, d, hop], ag_recv.at[k, d, hop], to)

    def come_chip(d, hop):
        return z - hop if d == 0 else z + hop

    def hop_start(k, d, hop):
        @pl.when(may_send(d, hop))
        def _():
            hop_copy(k, d, hop).start()

    def own_pass(k):
        return shard_send(k, z, c, agf_send.at[k, 0, 0], agf_recv.at[k, 0, 0], other)

    def come_pass(k, d, hop, core):
        return shard_send(k, come_chip(d, hop), core, agf_send.at[k, d, hop],
                          agf_recv.at[k, d, hop], other)

    def gather_start(k):
        for d in range(2):
            hop_start(k, d, 1)
        own_pass(k).start()

    def gather_hop(k, hop):
        for d in range(2):
            @pl.when(has_come(d, hop))
            def _():
                shard_send(k, come_chip(d, hop), c, ag_send.at[k, d, hop],
                           ag_recv.at[k, d, hop], other).wait_recv()
                if hop + 1 < nz:
                    hop_start(k, d, hop + 1)
                come_pass(k, d, hop, c).start()

    def gather_finish(k):
        own_pass(k).wait_recv()
        for hop in range(1, nz):
            for d in range(2):
                @pl.when(has_come(d, hop))
                def _():
                    come_pass(k, d, hop, 1 - c).wait_recv()

    def gather_close(k):
        own_pass(k).wait_send()
        for hop in range(1, nz):
            for d in range(2):
                @pl.when(may_send(d, hop))
                def _():
                    hop_copy(k, d, hop).wait_send()

                @pl.when(has_come(d, hop))
                def _():
                    come_pass(k, d, hop, c).wait_send()

    def halo(f, buf, go):
        lower = send(buf.at[1, span(1)], buf.at[1, span(ext - 1)],
                     halo_send.at[f, 0], halo_recv.at[f, 0], q, (s + n - 1) % n)
        upper = send(buf.at[1, span(rows)], buf.at[1, span(0)],
                     halo_send.at[f, 1], halo_recv.at[f, 1], q, (s + 1) % n)
        if go:
            @pl.when(s > 0)
            def _():
                lower.start()

            @pl.when(s < n - 1)
            def _():
                upper.start()
        else:
            @pl.when(s < n - 1)
            def _():
                lower.wait_recv()

            @pl.when(s > 0)
            def _():
                upper.wait_recv()

            @pl.when(s > 0)
            def _():
                lower.wait_send()

            @pl.when(s < n - 1)
            def _():
                upper.wait_send()

            @pl.when(s == 0)
            def _():
                buf[1, span(0), :] = jnp.zeros((cols, chans), BF16)

            @pl.when(s == n - 1)
            def _():
                buf[1, span(ext - 1), :] = jnp.zeros((cols, chans), BF16)

    def sides(buf, r, v):
        col = lax.broadcasted_iota(jnp.int32, (cols, chans), 0)
        left = jnp.where(col == 0, 0.0, pltpu.roll(v, 1, 0)).astype(BF16)
        right = jnp.where(col == cols - 1, 0.0, pltpu.roll(v, cols - 1, 0)).astype(BF16)
        buf[0, span(r), :] = left
        buf[2, span(r), :] = right
        return left, right

    gather_start(0)

    mask_t = jnp.transpose(mask_ref[...].astype(F32))

    def mask_row(r):
        c_in[r].wait()
        v = cot[pl.ds(r * cols, cols), :].astype(F32) * mask_t[:, r:r + 1]
        ms[1, pl.ds((r + 1) * cols, cols), :] = v.astype(BF16)

    mb[...] = mom_ref[...].astype(BF16)
    for level in range(levels):
        to = (q + (1 << level)) % reps
        for j, (src, dst) in enumerate(((wb, gw), (mb, gm))):
            cp = send(src, dst.at[level], go_send.at[j, level], go_recv.at[j, level], to, s)
            cp.start()
            started.append(cp)
    early = started[-2 * levels:]

    for r in order:
        mask_row(r)
    gather_hop(0, 1)
    for r in order:
        x_in[r].wait()

    def prep_x(r, offsets):
        v = xs[1, span(r), :]
        flat = jnp.transpose(v)
        for i in offsets:
            x_t[pl.ds(i * chans, chans), span(r - i)] = flat
        sides(xs, r, v.astype(F32))

    def prep_m(r):
        v = ms[1, span(r), :]
        left, right = sides(ms, r, v.astype(F32))
        for i, part in enumerate((left, v, right)):
            m_t[pl.ds(i * chans, chans), span(r)] = jnp.transpose(part)

    @pl.loop(2, rows)
    def _(r):
        prep_x(r, (0, 1, 2))

    prep_x(1, (0, 1))
    prep_x(rows, (1, 2))
    if nz > 2:
        gather_hop(0, 2)

    @pl.loop(1, rows + 1)
    def _(r):
        prep_m(r)

    for hop in range(3, nz):
        gather_hop(0, hop)
    halo(0, xs, True)
    halo(1, ms, True)
    gather_start(1)
    gather_finish(0)

    def conv(buf, ker, h, ahead):
        parts = []
        for i in range(3):
            for j in range(3):
                a, b = (i, j) if ahead else (2 - i, 2 - j)
                parts.append(buf[b, span(h + a, 2), :])
        return jnp.dot(jnp.concatenate(parts, axis=1), ker[...], preferred_element_type=F32)

    def turn(k):
        @pl.loop(0, taps)
        def _(t):
            at = pl.ds(pl.multiple_of(t * chans, chans), chans)
            k_t[k, at, :] = jnp.transpose(kf[k, at, :])

    def ahead(h):
        pre = conv(xs, kf.at[0], h, True)
        sig = 1.0 / (1.0 + jnp.exp(-pre))
        slope[span(h, 2), :] = sig * (1.0 + pre * (1.0 - sig))
        hid[span(h, 2), :] = (pre * sig).astype(BF16)

    @pl.loop(2, rows - 2, step=2, unroll=2)
    def _(h):
        ahead(h)

    gather_hop(1, 1)
    halo(0, xs, False)
    prep_x(0, (0,))
    prep_x(ext - 1, (2,))

    @pl.loop(0, 2, unroll=2)
    def _(t):
        ahead(t * (rows - 2))

    if nz > 2:
        gather_hop(1, 2)
    halo(1, ms, False)
    prep_m(0)
    prep_m(ext - 1)

    def put_grad(k, tap, g):
        gb[k, pl.ds(pl.multiple_of(tap * chans, chans), chans), :] = (g * scale).astype(BF16)

    ends_first = sorted(range(nz), key=lambda y: (min(y, nz - 1 - y), y))

    def share_copy(k, y):
        return send(gb.at[k, shard_rows(2 * y + 1 - c)], sib.at[k, y],
                    rs1_send.at[k, y], rs1_recv.at[k, y], q, other)

    def share_start(k, chips):
        for y in chips:
            cp = share_copy(k, y)
            cp.start()
            started.append(cp)

    def far_copy(k, y):
        return send(pair.at[k, y], far.at[k, z], rs2_send.at[k, y], rs2_recv.at[k, z],
                    q, y * 2 + c)

    def share_pass(k, chips):
        for y in chips:
            share_copy(k, y).wait_recv()
            both = gb[k, shard_rows(2 * y + c), :].astype(F32) + sib[k, y].astype(F32)
            pair[k, y] = both.astype(BF16)

            @pl.when(z != y)
            def _():
                far_copy(k, y).start()

    def share_close(k):
        for o in range(1, nz):
            far_copy(k, (z + o) % nz).wait_send()

    def share_finish(k):
        total = pair[k, z].astype(F32)
        for o in range(1, nz):
            y = (z + o) % nz
            send(pair.at[k, y], far.at[k, y], rs2_send.at[k, y], rs2_recv.at[k, y],
                 q, y * 2 + c).wait_recv()
            total = total + far[k, y].astype(F32)
        gk[k] = total.astype(BF16)
        nm_ref[k] = total
        out = []
        for level in range(levels):
            cp = send(gk.at[k], gg.at[k, level], go_send.at[2 + k, level], go_recv.at[2 + k, level],
                      (q + (1 << level)) % reps, s)
            cp.start()
            out.append(cp)
        started.extend(out)
        return out

    def settle(k, copies):
        for cp in copies:
            cp.wait_recv()
        g_in = jnp.zeros((sh, chans), F32)
        m_in = jnp.zeros((sh, chans), F32)
        w_in = jnp.zeros((sh, chans), F32)
        for level in range(levels):
            g_in = g_in + coef[level] * gg[k, level].astype(F32)
            m_in = m_in + coef[level] * gm[level, k].astype(F32)
            w_in = w_in + coef[level] * gw[level, k].astype(F32)
        mixed = 0.5 * (0.9 * (mom_ref[k] + m_in) + nm_ref[k] + g_in)
        nm_ref[k] = mixed
        nw_ref[k] = 0.5 * (w_ref[k] + w_in) - 0.01 * mixed

    for i in (1, 0, 2):
        g = jnp.dot(m_t[:, (2 - i) * cols:(2 - i + rows) * cols], hid[...],
                    preferred_element_type=F32)
        for j in range(3):
            put_grad(1, 3 * i + j, jnp.transpose(g[(2 - j) * chans:(3 - j) * chans]))
        if i == 1:
            for hop in range(3, nz):
                gather_hop(1, hop)

    share_start(1, ends_first)
    gather_finish(1)
    turn(1)

    def back(h):
        v = conv(ms, k_t.at[1], h, False) * slope[span(h, 2), :]
        ps[1, span(h + 1, 2), :] = v.astype(BF16)
        sides(ps, h + 1, v[:cols])
        sides(ps, h + 2, v[cols:])

    @pl.loop(0, 2, unroll=2)
    def _(t):
        back(t * (rows - 2))

    halo(2, ps, True)
    share_pass(1, ends_first)

    @pl.loop(2, rows - 2, step=2, unroll=2)
    def _(h):
        back(h)

    done, sent, passed = set(), [], []
    for i in (0, 2, 1):
        for j in range(3):
            put_grad(0, 3 * i + j, jnp.dot(
                x_t[i * chans:(i + 1) * chans, :], ps[2 - j, cols:(rows + 1) * cols, :],
                preferred_element_type=F32))
            done.add(3 * i + j)
        share_pass(0, [y for y in sent if y not in passed])
        passed = list(sent)
        ready = [y for y in ends_first if y not in sent and all(
            tap in done for tap in range(2 * y * sh // chans, (2 * (y + 1) * sh - 1) // chans + 1))]
        share_start(0, ready)
        sent = sent + ready

    turn(0)
    share_pass(0, [y for y in sent if y not in passed])

    def out_row(h):
        v = conv(ps, k_t.at[0], h, False) + ms[1, span(h + 1, 2), :].astype(F32)
        cot[span(h, 2), :] = v.astype(BF16)

    halo(2, ps, False)
    sides(ps, 0, ps[1, span(0), :].astype(F32))
    sides(ps, ext - 1, ps[1, span(ext - 1), :].astype(F32))
    half = rows // 2

    @pl.loop(0, half, step=2, unroll=2)
    def _(h):
        out_row(h)

    last1 = share_finish(1)

    @pl.loop(half, rows, step=2, unroll=2)
    def _(h):
        out_row(h)

    stores = [pltpu.make_async_copy(cot.at[pl.ds(r * cols, cols)], gi_hbm.at[r], loc_sem.at[r])
              for r in range(rows)]
    for cp in stores:
        cp.start()
    for cp in early:
        cp.wait_recv()
    last0 = share_finish(0)
    settle(1, last1)
    settle(0, last0)
    for cp in stores:
        cp.wait()
    for cp in started:
        cp.wait_send()
    for k in range(2):
        gather_close(k)
        share_close(k)


def copy_kernel(gi, nw, nm, gi_out, nw_out, nm_out, gi_at, w_at, m_at, came, left):
    rows = gi.shape[0]
    moves = [(gi.at[r], gi_at.at[r], gi_out.at[r]) for r in range(rows)]
    moves += [(nw.at[k], w_at.at[k], nw_out.at[k]) for k in range(2)]
    moves += [(nm.at[k], m_at.at[k], nm_out.at[k]) for k in range(2)]
    loads = [pltpu.make_async_copy(a, b, came.at[i]) for i, (a, b, _) in enumerate(moves)]
    stores = [pltpu.make_async_copy(b, d, left.at[i]) for i, (_, b, d) in enumerate(moves)]
    for cp in loads:
        cp.start()
    for a, b in zip(loads, stores):
        a.wait()
        b.start()
    for cp in stores:
        cp.wait()


def shards(inputs, cotangent, land_mask, weights, momentum, step):
    n = lax.axis_size("space")
    reps = lax.axis_size("replica")
    levels = reps.bit_length() - 1
    rows, cols, chans = inputs.shape[1:]
    sh = weights.shape[2]
    kc = sh * n
    ext = rows + 2
    nz = n // 2
    scale = 1.0 / math.sqrt(rows * n * cols)
    coef = (step[0] % levels == jnp.arange(levels)).astype(F32)
    vm = pltpu.VMEM
    sem = pltpu.SemaphoreType.DMA
    flops = 5 * 2 * rows * cols * kc * chans
    any_space = pl.BlockSpec(memory_space=pl.ANY)
    in_vmem = pl.BlockSpec(memory_space=pltpu.VMEM)
    gi, nw, nm = pl.pallas_call(
        partial(block_kernel, n, reps, levels, scale),
        out_shape=(
            jax.ShapeDtypeStruct((rows, cols, chans), BF16),
            jax.ShapeDtypeStruct((2, sh, chans), F32),
            jax.ShapeDtypeStruct((2, sh, chans), F32),
        ),
        in_specs=[pl.BlockSpec(memory_space=pltpu.SMEM), any_space, any_space,
                  in_vmem, in_vmem, in_vmem],
        out_specs=(any_space, in_vmem, in_vmem),
        scratch_shapes=[
            vm((3, ext * cols, chans), BF16),
            vm((3, ext * cols, chans), BF16),
            vm((3, ext * cols, chans), BF16),
            vm((3 * chans, rows * cols), BF16),
            vm((3 * chans, ext * cols), BF16),
            vm((rows * cols, chans), BF16),
            vm((rows * cols, chans), F32),
            vm((rows * cols, chans), BF16),
            vm((2, kc, chans), BF16),
            vm((2, kc, chans), BF16),
            vm((2, sh, chans), BF16),
            vm((2, sh, chans), BF16),
            vm((2, kc, chans), BF16),
            vm((2, nz, sh, chans), BF16),
            vm((2, nz, sh, chans), BF16),
            vm((2, nz, sh, chans), BF16),
            vm((2, sh, chans), BF16),
            vm((levels, 2, sh, chans), BF16),
            vm((levels, 2, sh, chans), BF16),
            vm((2, levels, sh, chans), BF16),
            sem((2 * rows,)),
            sem((3, 2)), sem((3, 2)),
            sem((2, 2, nz)), sem((2, 2, nz)), sem((2, 2, nz)), sem((2, 2, nz)),
            sem((2, nz)), sem((2, nz)), sem((2, nz)), sem((2, nz)),
            sem((4, levels)), sem((4, levels)),
        ],
        compiler_params=pltpu.CompilerParams(
            collective_id=0, has_side_effects=True, vmem_limit_bytes=63 * 1024 * 1024),
        cost_estimate=pl.CostEstimate(flops=flops, bytes_accessed=12 << 20, transcendentals=0),
    )(coef, inputs[0], cotangent[0], land_mask, weights[0], momentum[0])
    gi, nw, nm = pl.pallas_call(
        copy_kernel,
        out_shape=tuple(jax.ShapeDtypeStruct(v.shape, v.dtype) for v in (gi, nw, nm)),
        in_specs=[any_space] * 3,
        out_specs=(any_space,) * 3,
        scratch_shapes=[vm(gi.shape, BF16), vm(nw.shape, F32), vm(nm.shape, F32),
                        sem((rows + 4,)), sem((rows + 4,))],
        compiler_params=pltpu.CompilerParams(vmem_limit_bytes=16 * 1024 * 1024),
    )(gi, nw, nm)
    return gi[None], nw[None], nm[None]


def solution(mesh):
    in_specs = (
        P("replica", "space", None, None),
        P("replica", "space", None, None),
        P("space", None),
        P("replica", None, "space", None),
        P("replica", None, "space", None),
        P(),
    )
    out_specs = (
        P("replica", "space", None, None),
        P("replica", None, "space", None),
        P("replica", None, "space", None),
    )
    return jax.shard_map(shards, mesh=mesh, in_specs=in_specs, out_specs=out_specs, check_vma=False)
```

```python
from functools import partial
import math

import jax
import jax.numpy as jnp
from jax import lax
from jax.experimental import pallas as pl
from jax.experimental.pallas import tpu as pltpu
from jax.sharding import PartitionSpec as P

F32 = jnp.float32
BF16 = jnp.bfloat16
MESH = pl.DeviceIdType.MESH


def block_kernel(
    n, reps, levels, scale,
    coef, x_hbm, cot_hbm, mask_ref, w_ref, mom_ref,
    gi_hbm, nw_ref, nm_ref,
    xs, ms, ps, x_t, h_t, slope, cot, kf, k_t, wb, mb, gb, sib, pair, far, gk, gw, gm, gg,
    loc_sem, halo_send, halo_recv, ag_send, ag_recv, agf_send, agf_recv,
    rs1_send, rs1_recv, rs2_send, rs2_recv, go_send, go_recv,
):
    rows, cols, chans = x_hbm.shape
    ext = rows + 2
    nz = n // 2
    sh = w_ref.shape[1]
    taps = 9
    q = lax.axis_index("replica")
    s = lax.axis_index("space")
    z = s // 2
    c = s % 2
    other = s + 1 - 2 * c

    def span(r, count=1):
        return pl.ds(pl.multiple_of(r * cols, cols), count * cols)

    def shard_rows(i):
        return pl.ds(pl.multiple_of(i * sh, 16), sh)

    def send(src, dst, ssem, rsem, rep, spc):
        return pltpu.make_async_remote_copy(
            src_ref=src, dst_ref=dst, send_sem=ssem, recv_sem=rsem,
            device_id=(rep, spc), device_id_type=MESH)

    started = []

    x_in = [pltpu.make_async_copy(x_hbm.at[r], xs.at[1, pl.ds((r + 1) * cols, cols)], loc_sem.at[r])
            for r in range(rows)]
    c_in = [pltpu.make_async_copy(cot_hbm.at[r], cot.at[pl.ds(r * cols, cols)], loc_sem.at[rows + r])
            for r in range(rows)]
    order = [0, rows - 1] + list(range(1, rows - 1))
    for r in order:
        x_in[r].start()
    for r in order:
        c_in[r].start()

    wb[...] = w_ref[...].astype(BF16)
    for k in range(2):
        kf[k, shard_rows(s), :] = w_ref[k].astype(BF16)

    barrier = pltpu.get_barrier_semaphore()
    for o in range(1, n):
        pl.semaphore_signal(barrier, inc=1, device_id=(q, (s + o) % n), device_id_type=MESH)
    for o in range(1, reps):
        pl.semaphore_signal(barrier, inc=1, device_id=((q + o) % reps, s), device_id_type=MESH)
    pl.semaphore_wait(barrier, n - 1 + reps - 1)

    def shard_send(k, chip, core, ssem, rsem, spc):
        at = shard_rows(2 * chip + core)
        return send(kf.at[k, at], kf.at[k, at], ssem, rsem, q, spc)

    def may_send(d, hop):
        if d == 0:
            return (z + 1 >= hop) & (z + 1 < nz)
        return (z + hop <= nz) & (z >= 1)

    def has_come(d, hop):
        return z >= hop if d == 0 else z + hop < nz

    def hop_copy(k, d, hop):
        chip = z + 1 - hop if d == 0 else z - 1 + hop
        to = s + 2 if d == 0 else s - 2
        return shard_send(k, chip, c, ag_send.at[k, d, hop], ag_recv.at[k, d, hop], to)

    def come_chip(d, hop):
        return z - hop if d == 0 else z + hop

    def hop_start(k, d, hop):
        @pl.when(may_send(d, hop))
        def _():
            hop_copy(k, d, hop).start()

    def own_pass(k):
        return shard_send(k, z, c, agf_send.at[k, 0, 0], agf_recv.at[k, 0, 0], other)

    def come_pass(k, d, hop, core):
        return shard_send(k, come_chip(d, hop), core, agf_send.at[k, d, hop],
                          agf_recv.at[k, d, hop], other)

    def gather_start(k):
        for d in range(2):
            hop_start(k, d, 1)
        own_pass(k).start()

    def gather_hop(k, hop):
        for d in range(2):
            @pl.when(has_come(d, hop))
            def _():
                shard_send(k, come_chip(d, hop), c, ag_send.at[k, d, hop],
                           ag_recv.at[k, d, hop], other).wait_recv()
                if hop + 1 < nz:
                    hop_start(k, d, hop + 1)
                come_pass(k, d, hop, c).start()

    def gather_finish(k):
        own_pass(k).wait_recv()
        for hop in range(1, nz):
            for d in range(2):
                @pl.when(has_come(d, hop))
                def _():
                    come_pass(k, d, hop, 1 - c).wait_recv()

    def gather_close(k):
        own_pass(k).wait_send()
        for hop in range(1, nz):
            for d in range(2):
                @pl.when(may_send(d, hop))
                def _():
                    hop_copy(k, d, hop).wait_send()

                @pl.when(has_come(d, hop))
                def _():
                    come_pass(k, d, hop, c).wait_send()

    def halo(f, buf, go):
        lower = send(buf.at[1, span(1)], buf.at[1, span(ext - 1)],
                     halo_send.at[f, 0], halo_recv.at[f, 0], q, (s + n - 1) % n)
        upper = send(buf.at[1, span(rows)], buf.at[1, span(0)],
                     halo_send.at[f, 1], halo_recv.at[f, 1], q, (s + 1) % n)
        if go:
            @pl.when(s > 0)
            def _():
                lower.start()

            @pl.when(s < n - 1)
            def _():
                upper.start()
        else:
            @pl.when(s < n - 1)
            def _():
                lower.wait_recv()

            @pl.when(s > 0)
            def _():
                upper.wait_recv()

            @pl.when(s > 0)
            def _():
                lower.wait_send()

            @pl.when(s < n - 1)
            def _():
                upper.wait_send()

            @pl.when(s == 0)
            def _():
                buf[1, span(0), :] = jnp.zeros((cols, chans), BF16)

            @pl.when(s == n - 1)
            def _():
                buf[1, span(ext - 1), :] = jnp.zeros((cols, chans), BF16)

    def sides(buf, r, v):
        col = lax.broadcasted_iota(jnp.int32, (cols, chans), 0)
        left = jnp.where(col == 0, 0.0, pltpu.roll(v, 1, 0)).astype(BF16)
        right = jnp.where(col == cols - 1, 0.0, pltpu.roll(v, cols - 1, 0)).astype(BF16)
        buf[0, span(r), :] = left
        buf[2, span(r), :] = right
        return left, right

    gather_start(0)

    mask_t = jnp.transpose(mask_ref[...].astype(F32))

    def mask_row(r):
        c_in[r].wait()
        v = cot[pl.ds(r * cols, cols), :].astype(F32) * mask_t[:, r:r + 1]
        ms[1, pl.ds((r + 1) * cols, cols), :] = v.astype(BF16)

    mb[...] = mom_ref[...].astype(BF16)
    for level in range(levels):
        to = (q + (1 << level)) % reps
        for j, (src, dst) in enumerate(((wb, gw), (mb, gm))):
            cp = send(src, dst.at[level], go_send.at[j, level], go_recv.at[j, level], to, s)
            cp.start()
            started.append(cp)
    early = started[-2 * levels:]

    for r in order:
        mask_row(r)
    gather_hop(0, 1)
    for r in order:
        x_in[r].wait()

    def prep_x(r):
        v = xs[1, span(r), :]
        x_t[:, span(r)] = jnp.transpose(v)
        sides(xs, r, v.astype(F32))

    def prep_m(r):
        sides(ms, r, ms[1, span(r), :].astype(F32))

    def edges(prep):
        @pl.loop(0, 2)
        def _(e):
            prep(e * (ext - 1))

    @pl.loop(1, rows + 1)
    def _(r):
        prep_x(r)

    if nz > 2:
        gather_hop(0, 2)

    @pl.loop(1, rows + 1)
    def _(r):
        prep_m(r)

    for hop in range(3, nz):
        gather_hop(0, hop)
    halo(0, xs, True)
    halo(1, ms, True)
    gather_start(1)
    gather_finish(0)

    def conv(buf, ker, h, ahead):
        parts = []
        for i in range(3):
            for j in range(3):
                a, b = (i, j) if ahead else (2 - i, 2 - j)
                parts.append(buf[b, span(h + a, 2), :])
        return jnp.dot(jnp.concatenate(parts, axis=1), ker[...], preferred_element_type=F32)

    def turn(k):
        @pl.loop(0, taps)
        def _(t):
            at = pl.ds(pl.multiple_of(t * chans, chans), chans)
            k_t[k, at, :] = jnp.transpose(kf[k, at, :])

    half = rows // 2

    @pl.loop(0, half)
    def _(e):
        @pl.when(e == half - 2)
        def _():
            gather_hop(1, 1)
            halo(0, xs, False)
            edges(prep_x)

        h = (2 * e + 2) % rows
        pre = conv(xs, kf.at[0], h, True)
        sig = 0.5 * jnp.tanh(0.5 * pre) + 0.5
        slope[span(h, 2), :] = sig * (1.0 + pre * (1.0 - sig))
        h_t[:, span(h, 2)] = jnp.transpose((pre * sig).astype(BF16))

    if nz > 2:
        gather_hop(1, 2)
    halo(1, ms, False)
    edges(prep_m)

    def put_grad(k, tap, g):
        gb[k, pl.ds(pl.multiple_of(tap * chans, chans), chans), :] = (g * scale).astype(BF16)

    ends_first = sorted(range(nz), key=lambda y: (min(y, nz - 1 - y), y))

    def share_copy(k, y):
        return send(gb.at[k, shard_rows(2 * y + 1 - c)], sib.at[k, y],
                    rs1_send.at[k, y], rs1_recv.at[k, y], q, other)

    def share_start(k, chips):
        for y in chips:
            share_copy(k, y).start()

    def far_copy(k, y):
        return send(pair.at[k, y], far.at[k, z], rs2_send.at[k, y], rs2_recv.at[k, z],
                    q, y * 2 + c)

    def share_pass(k, chips):
        for y in chips:
            share_copy(k, y).wait_recv()
            both = gb[k, shard_rows(2 * y + c), :].astype(F32) + sib[k, y].astype(F32)
            pair[k, y] = both.astype(BF16)

            @pl.when(z != y)
            def _():
                far_copy(k, y).start()

    def share_close(k):
        for y in range(nz):
            share_copy(k, y).wait_send()
        for o in range(1, nz):
            far_copy(k, (z + o) % nz).wait_send()

    def gossip_copy(k, level):
        return send(gk.at[k], gg.at[k, level], go_send.at[2 + k, level], go_recv.at[2 + k, level],
                    (q + (1 << level)) % reps, s)

    def share_finish(k):
        total = pair[k, z].astype(F32)
        for o in range(1, nz):
            y = (z + o) % nz
            send(pair.at[k, y], far.at[k, y], rs2_send.at[k, y], rs2_recv.at[k, y],
                 q, y * 2 + c).wait_recv()
            total = total + far[k, y].astype(F32)
        gk[k] = total.astype(BF16)
        nm_ref[k] = total
        for level in range(levels):
            gossip_copy(k, level).start()

    def settle(k):
        for level in range(levels):
            gossip_copy(k, level).wait_recv()
        g_in = jnp.zeros((sh, chans), F32)
        m_in = jnp.zeros((sh, chans), F32)
        w_in = jnp.zeros((sh, chans), F32)
        for level in range(levels):
            g_in = g_in + coef[level] * gg[k, level].astype(F32)
            m_in = m_in + coef[level] * gm[level, k].astype(F32)
            w_in = w_in + coef[level] * gw[level, k].astype(F32)
        mixed = 0.5 * (0.9 * (mom_ref[k] + m_in) + nm_ref[k] + g_in)
        nm_ref[k] = mixed
        nw_ref[k] = 0.5 * (w_ref[k] + w_in) - 0.01 * mixed

    @pl.loop(0, taps)
    def _(tap):
        @pl.when(tap == 3)
        def _():
            for hop in range(3, nz):
                gather_hop(1, hop)

        put_grad(1, tap, jnp.dot(h_t[...], ms[2 - tap % 3, span(2 - tap // 3, rows), :],
                                 preferred_element_type=F32))

    share_start(1, ends_first)
    gather_finish(1)
    turn(1)

    @pl.loop(0, half)
    def _(e):
        h = (2 * e + rows - 2) % rows
        v = conv(ms, k_t.at[1], h, False) * slope[span(h, 2), :]
        ps[1, span(h + 1, 2), :] = v.astype(BF16)
        sides(ps, h + 1, v[:cols])
        sides(ps, h + 2, v[cols:])

        @pl.when(e == 1)
        def _():
            halo(2, ps, True)
            share_pass(1, ends_first)

    done, sent, plan = set(), [], []
    for i in (0, 2, 1):
        done.update((3 * i, 3 * i + 1, 3 * i + 2))
        ready = [y for y in ends_first if y not in sent and all(
            tap in done for tap in range(2 * y * sh // chans, (2 * (y + 1) * sh - 1) // chans + 1))]
        plan.append(ready)
        sent = sent + ready

    @pl.loop(0, taps)
    def _(e):
        @pl.when(e == 3)
        def _():
            share_start(0, plan[0])

        @pl.when(e == 6)
        def _():
            share_start(0, plan[1])
            share_pass(0, plan[0])

        i = (2 * (e // 3)) % 3
        j = e % 3
        put_grad(0, 3 * i + j, jnp.dot(x_t[:, span(i, rows)], ps[2 - j, span(1, rows), :],
                                       preferred_element_type=F32))

    share_start(0, plan[2])
    share_pass(0, plan[1])
    turn(0)
    share_pass(0, plan[2])

    @pl.loop(0, half)
    def _(e):
        @pl.when(e == half - 2)
        def _():
            halo(2, ps, False)
            edges(lambda r: sides(ps, r, ps[1, span(r), :].astype(F32)))
            share_finish(1)

        h = (2 * e + 2) % rows
        v = conv(ps, k_t.at[0], h, False) + ms[1, span(h + 1, 2), :].astype(F32)
        cot[span(h, 2), :] = v.astype(BF16)

    stores = [pltpu.make_async_copy(cot.at[pl.ds(r * cols, cols)], gi_hbm.at[r], loc_sem.at[r])
              for r in range(rows)]
    for cp in stores:
        cp.start()
    for cp in early:
        cp.wait_recv()
    share_finish(0)
    settle(1)
    settle(0)
    for cp in stores:
        cp.wait()
    for cp in started:
        cp.wait_send()
    for k in range(2):
        gather_close(k)
        share_close(k)
        for level in range(levels):
            gossip_copy(k, level).wait_send()


def copy_kernel(gi, nw, nm, gi_out, nw_out, nm_out, gi_at, w_at, m_at, came, left):
    rows = gi.shape[0]
    moves = [(gi.at[r], gi_at.at[r], gi_out.at[r]) for r in range(rows)]
    moves += [(nw.at[k], w_at.at[k], nw_out.at[k]) for k in range(2)]
    moves += [(nm.at[k], m_at.at[k], nm_out.at[k]) for k in range(2)]
    loads = [pltpu.make_async_copy(a, b, came.at[i]) for i, (a, b, _) in enumerate(moves)]
    stores = [pltpu.make_async_copy(b, d, left.at[i]) for i, (_, b, d) in enumerate(moves)]
    for cp in loads:
        cp.start()
    for a, b in zip(loads, stores):
        a.wait()
        b.start()
    for cp in stores:
        cp.wait()


def shards(inputs, cotangent, land_mask, weights, momentum, step):
    n = lax.axis_size("space")
    reps = lax.axis_size("replica")
    levels = reps.bit_length() - 1
    rows, cols, chans = inputs.shape[1:]
    sh = weights.shape[2]
    kc = sh * n
    ext = rows + 2
    nz = n // 2
    scale = 1.0 / math.sqrt(rows * n * cols)
    coef = (step[0] % levels == jnp.arange(levels)).astype(F32)
    vm = pltpu.VMEM
    sem = pltpu.SemaphoreType.DMA
    flops = 5 * 2 * rows * cols * kc * chans
    any_space = pl.BlockSpec(memory_space=pl.ANY)
    in_vmem = pl.BlockSpec(memory_space=pltpu.VMEM)
    gi, nw, nm = pl.pallas_call(
        partial(block_kernel, n, reps, levels, scale),
        out_shape=(
            jax.ShapeDtypeStruct((rows, cols, chans), BF16),
            jax.ShapeDtypeStruct((2, sh, chans), F32),
            jax.ShapeDtypeStruct((2, sh, chans), F32),
        ),
        in_specs=[pl.BlockSpec(memory_space=pltpu.SMEM), any_space, any_space,
                  in_vmem, in_vmem, in_vmem],
        out_specs=(any_space, in_vmem, in_vmem),
        scratch_shapes=[
            vm((3, ext * cols, chans), BF16),
            vm((3, ext * cols, chans), BF16),
            vm((3, ext * cols, chans), BF16),
            vm((chans, ext * cols), BF16),
            vm((chans, rows * cols), BF16),
            vm((rows * cols, chans), F32),
            vm((rows * cols, chans), BF16),
            vm((2, kc, chans), BF16),
            vm((2, kc, chans), BF16),
            vm((2, sh, chans), BF16),
            vm((2, sh, chans), BF16),
            vm((2, kc, chans), BF16),
            vm((2, nz, sh, chans), BF16),
            vm((2, nz, sh, chans), BF16),
            vm((2, nz, sh, chans), BF16),
            vm((2, sh, chans), BF16),
            vm((levels, 2, sh, chans), BF16),
            vm((levels, 2, sh, chans), BF16),
            vm((2, levels, sh, chans), BF16),
            sem((2 * rows,)),
            sem((3, 2)), sem((3, 2)),
            sem((2, 2, nz)), sem((2, 2, nz)), sem((2, 2, nz)), sem((2, 2, nz)),
            sem((2, nz)), sem((2, nz)), sem((2, nz)), sem((2, nz)),
            sem((4, levels)), sem((4, levels)),
        ],
        compiler_params=pltpu.CompilerParams(
            collective_id=0, has_side_effects=True, vmem_limit_bytes=63 * 1024 * 1024),
        cost_estimate=pl.CostEstimate(flops=flops, bytes_accessed=12 << 20, transcendentals=0),
    )(coef, inputs[0], cotangent[0], land_mask, weights[0], momentum[0])
    gi, nw, nm = pl.pallas_call(
        copy_kernel,
        out_shape=tuple(jax.ShapeDtypeStruct(v.shape, v.dtype) for v in (gi, nw, nm)),
        in_specs=[any_space] * 3,
        out_specs=(any_space,) * 3,
        scratch_shapes=[vm(gi.shape, BF16), vm(nw.shape, F32), vm(nm.shape, F32),
                        sem((rows + 4,)), sem((rows + 4,))],
        compiler_params=pltpu.CompilerParams(vmem_limit_bytes=63 * 1024 * 1024),
    )(gi, nw, nm)
    return gi[None], nw[None], nm[None]


def solution(mesh):
    in_specs = (
        P("replica", "space", None, None),
        P("replica", "space", None, None),
        P("space", None),
        P("replica", None, "space", None),
        P("replica", None, "space", None),
        P(),
    )
    out_specs = (
        P("replica", "space", None, None),
        P("replica", None, "space", None),
        P("replica", None, "space", None),
    )
    return jax.shard_map(shards, mesh=mesh, in_specs=in_specs, out_specs=out_specs, check_vma=False)
```

```python
from functools import partial
import math

import jax
import jax.numpy as jnp
from jax import lax
from jax.experimental import pallas as pl
from jax.experimental.pallas import tpu as pltpu
from jax.sharding import PartitionSpec as P

F32 = jnp.float32
BF16 = jnp.bfloat16
MESH = pl.DeviceIdType.MESH


def block_kernel(
    n, reps, levels, scale,
    coef, x_hbm, cot_hbm, mask_ref, w_ref, mom_ref,
    gi_hbm, nw_ref, nm_ref,
    xs, ms, ps, x_t, h_t, slope, cot, kf, k_t, wb, mb, gb, sib, pair, far, gk, gw, gm, gg,
    loc_sem, halo_send, halo_recv, ag_send, ag_recv, agf_send, agf_recv,
    rs1_send, rs1_recv, rs2_send, rs2_recv, go_send, go_recv,
):
    rows, cols, chans = x_hbm.shape
    ext = rows + 2
    nz = n // 2
    sh = w_ref.shape[1]
    taps = 9
    q = lax.axis_index("replica")
    s = lax.axis_index("space")
    z = s // 2
    c = s % 2
    other = s + 1 - 2 * c

    def span(r, count=1):
        return pl.ds(pl.multiple_of(r * cols, cols), count * cols)

    def shard_rows(i):
        return pl.ds(pl.multiple_of(i * sh, 16), sh)

    def send(src, dst, ssem, rsem, rep, spc):
        return pltpu.make_async_remote_copy(
            src_ref=src, dst_ref=dst, send_sem=ssem, recv_sem=rsem,
            device_id=(rep, spc), device_id_type=MESH)

    started = []

    x_in = [pltpu.make_async_copy(x_hbm.at[r], xs.at[1, pl.ds((r + 1) * cols, cols)], loc_sem.at[r])
            for r in range(rows)]
    c_in = [pltpu.make_async_copy(cot_hbm.at[r], cot.at[pl.ds(r * cols, cols)], loc_sem.at[rows + r])
            for r in range(rows)]
    order = [0, rows - 1] + list(range(1, rows - 1))
    for r in order:
        x_in[r].start()
    for r in order:
        c_in[r].start()

    wb[...] = w_ref[...].astype(BF16)
    for k in range(2):
        kf[k, shard_rows(s), :] = w_ref[k].astype(BF16)

    barrier = pltpu.get_barrier_semaphore()
    for o in range(1, n):
        pl.semaphore_signal(barrier, inc=1, device_id=(q, (s + o) % n), device_id_type=MESH)
    for o in range(1, reps):
        pl.semaphore_signal(barrier, inc=1, device_id=((q + o) % reps, s), device_id_type=MESH)
    pl.semaphore_wait(barrier, n - 1 + reps - 1)

    def shard_send(k, chip, core, ssem, rsem, spc):
        at = shard_rows(2 * chip + core)
        return send(kf.at[k, at], kf.at[k, at], ssem, rsem, q, spc)

    def may_send(d, hop):
        if d == 0:
            return (z + 1 >= hop) & (z + 1 < nz)
        return (z + hop <= nz) & (z >= 1)

    def has_come(d, hop):
        return z >= hop if d == 0 else z + hop < nz

    def hop_copy(k, d, hop):
        chip = z + 1 - hop if d == 0 else z - 1 + hop
        to = s + 2 if d == 0 else s - 2
        return shard_send(k, chip, c, ag_send.at[k, d, hop], ag_recv.at[k, d, hop], to)

    def come_chip(d, hop):
        return z - hop if d == 0 else z + hop

    def hop_start(k, d, hop):
        @pl.when(may_send(d, hop))
        def _():
            hop_copy(k, d, hop).start()

    def own_pass(k):
        return shard_send(k, z, c, agf_send.at[k, 0, 0], agf_recv.at[k, 0, 0], other)

    def come_pass(k, d, hop, core):
        return shard_send(k, come_chip(d, hop), core, agf_send.at[k, d, hop],
                          agf_recv.at[k, d, hop], other)

    def gather_start(k):
        for d in range(2):
            hop_start(k, d, 1)
        own_pass(k).start()

    def gather_hop(k, hop):
        for d in range(2):
            @pl.when(has_come(d, hop))
            def _():
                shard_send(k, come_chip(d, hop), c, ag_send.at[k, d, hop],
                           ag_recv.at[k, d, hop], other).wait_recv()
                if hop + 1 < nz:
                    hop_start(k, d, hop + 1)
                come_pass(k, d, hop, c).start()

    def gather_finish(k):
        own_pass(k).wait_recv()
        for hop in range(1, nz):
            for d in range(2):
                @pl.when(has_come(d, hop))
                def _():
                    come_pass(k, d, hop, 1 - c).wait_recv()

    def gather_close(k):
        own_pass(k).wait_send()
        for hop in range(1, nz):
            for d in range(2):
                @pl.when(may_send(d, hop))
                def _():
                    hop_copy(k, d, hop).wait_send()

                @pl.when(has_come(d, hop))
                def _():
                    come_pass(k, d, hop, c).wait_send()

    def halo(f, buf, go):
        lower = send(buf.at[1, span(1)], buf.at[1, span(ext - 1)],
                     halo_send.at[f, 0], halo_recv.at[f, 0], q, (s + n - 1) % n)
        upper = send(buf.at[1, span(rows)], buf.at[1, span(0)],
                     halo_send.at[f, 1], halo_recv.at[f, 1], q, (s + 1) % n)
        if go:
            @pl.when(s > 0)
            def _():
                lower.start()

            @pl.when(s < n - 1)
            def _():
                upper.start()
        else:
            @pl.when(s < n - 1)
            def _():
                lower.wait_recv()

            @pl.when(s > 0)
            def _():
                upper.wait_recv()

            @pl.when(s > 0)
            def _():
                lower.wait_send()

            @pl.when(s < n - 1)
            def _():
                upper.wait_send()

            @pl.when(s == 0)
            def _():
                buf[1, span(0), :] = jnp.zeros((cols, chans), BF16)

            @pl.when(s == n - 1)
            def _():
                buf[1, span(ext - 1), :] = jnp.zeros((cols, chans), BF16)

    def sides(buf, r, v):
        col = lax.broadcasted_iota(jnp.int32, (cols, chans), 0)
        left = jnp.where(col == 0, 0.0, pltpu.roll(v, 1, 0)).astype(BF16)
        right = jnp.where(col == cols - 1, 0.0, pltpu.roll(v, cols - 1, 0)).astype(BF16)
        buf[0, span(r), :] = left
        buf[2, span(r), :] = right
        return left, right

    gather_start(0)

    mask_t = jnp.transpose(mask_ref[...].astype(F32))

    def mask_row(r):
        c_in[r].wait()
        v = cot[pl.ds(r * cols, cols), :].astype(F32) * mask_t[:, r:r + 1]
        ms[1, pl.ds((r + 1) * cols, cols), :] = v.astype(BF16)

    for r in order:
        mask_row(r)
    gather_hop(0, 1)
    for r in order:
        x_in[r].wait()

    def prep_x(r):
        v = xs[1, span(r), :]
        x_t[:, span(r)] = jnp.transpose(v)
        sides(xs, r, v.astype(F32))

    def prep_m(r):
        sides(ms, r, ms[1, span(r), :].astype(F32))

    def edges(prep):
        @pl.loop(0, 2)
        def _(e):
            prep(e * (ext - 1))

    @pl.loop(1, rows + 1)
    def _(r):
        prep_x(r)

    if nz > 2:
        gather_hop(0, 2)

    @pl.loop(1, rows + 1)
    def _(r):
        prep_m(r)

    for hop in range(3, nz):
        gather_hop(0, hop)
    halo(0, xs, True)
    halo(1, ms, True)
    gather_start(1)
    gather_finish(0)

    def conv(buf, ker, h, ahead, count=2):
        parts = []
        for i in range(3):
            for j in range(3):
                a, b = (i, j) if ahead else (2 - i, 2 - j)
                parts.append(buf[b, span(h + a, count), :])
        return jnp.dot(jnp.concatenate(parts, axis=1), ker[...], preferred_element_type=F32)

    def turn(k):
        @pl.loop(0, taps)
        def _(t):
            at = pl.ds(pl.multiple_of(t * chans, chans), chans)
            k_t[k, at, :] = jnp.transpose(kf[k, at, :])

    half = rows // 2

    @pl.loop(0, half)
    def _(e):
        @pl.when(e == half - 2)
        def _():
            gather_hop(1, 1)
            halo(0, xs, False)
            edges(prep_x)

        h = (2 * e + 2) % rows
        for r in (h, h + 1):
            pre = conv(xs, kf.at[0], r, True, 1)
            sig = 0.5 * jnp.tanh(0.5 * pre) + 0.5
            slope[span(r), :] = sig * (1.0 + pre * (1.0 - sig))
            h_t[:, span(r)] = jnp.transpose((pre * sig).astype(BF16))

    mb[...] = mom_ref[...].astype(BF16)
    for level in range(levels):
        to = (q + (1 << level)) % reps
        for j, (src, dst) in enumerate(((wb, gw), (mb, gm))):
            cp = send(src, dst.at[level], go_send.at[j, level], go_recv.at[j, level], to, s)
            cp.start()
            started.append(cp)
    early = started[-2 * levels:]

    if nz > 2:
        gather_hop(1, 2)
    halo(1, ms, False)
    edges(prep_m)

    def put_grad(k, tap, g):
        gb[k, pl.ds(pl.multiple_of(tap * chans, chans), chans), :] = (g * scale).astype(BF16)

    ends_first = sorted(range(nz), key=lambda y: (min(y, nz - 1 - y), y))

    def share_copy(k, y):
        return send(gb.at[k, shard_rows(2 * y + 1 - c)], sib.at[k, y],
                    rs1_send.at[k, y], rs1_recv.at[k, y], q, other)

    def share_start(k, chips):
        for y in chips:
            share_copy(k, y).start()

    def far_copy(k, y):
        return send(pair.at[k, y], far.at[k, z], rs2_send.at[k, y], rs2_recv.at[k, z],
                    q, y * 2 + c)

    def share_pass(k, chips):
        for y in chips:
            share_copy(k, y).wait_recv()
            both = gb[k, shard_rows(2 * y + c), :].astype(F32) + sib[k, y].astype(F32)
            pair[k, y] = both.astype(BF16)

            @pl.when(z != y)
            def _():
                far_copy(k, y).start()

    def share_close(k):
        for y in range(nz):
            share_copy(k, y).wait_send()
        for o in range(1, nz):
            far_copy(k, (z + o) % nz).wait_send()

    def gossip_copy(k, level):
        return send(gk.at[k], gg.at[k, level], go_send.at[2 + k, level], go_recv.at[2 + k, level],
                    (q + (1 << level)) % reps, s)

    def share_finish(k):
        total = pair[k, z].astype(F32)
        for o in range(1, nz):
            y = (z + o) % nz
            send(pair.at[k, y], far.at[k, y], rs2_send.at[k, y], rs2_recv.at[k, y],
                 q, y * 2 + c).wait_recv()
            total = total + far[k, y].astype(F32)
        gk[k] = total.astype(BF16)
        nm_ref[k] = total
        for level in range(levels):
            gossip_copy(k, level).start()

    def settle(k):
        for level in range(levels):
            gossip_copy(k, level).wait_recv()
        g_in = jnp.zeros((sh, chans), F32)
        m_in = jnp.zeros((sh, chans), F32)
        w_in = jnp.zeros((sh, chans), F32)
        for level in range(levels):
            g_in = g_in + coef[level] * gg[k, level].astype(F32)
            m_in = m_in + coef[level] * gm[level, k].astype(F32)
            w_in = w_in + coef[level] * gw[level, k].astype(F32)
        mixed = 0.5 * (0.9 * (mom_ref[k] + m_in) + nm_ref[k] + g_in)
        nm_ref[k] = mixed
        nw_ref[k] = 0.5 * (w_ref[k] + w_in) - 0.01 * mixed

    @pl.loop(0, taps)
    def _(tap):
        @pl.when(tap == 3)
        def _():
            for hop in range(3, nz):
                gather_hop(1, hop)

        put_grad(1, tap, jnp.dot(h_t[...], ms[2 - tap % 3, span(2 - tap // 3, rows), :],
                                 preferred_element_type=F32))

    share_start(1, ends_first)
    gather_finish(1)
    turn(1)

    @pl.loop(0, half)
    def _(e):
        h = (2 * e + rows - 2) % rows
        for r in (h, h + 1):
            v = conv(ms, k_t.at[1], r, False, 1) * slope[span(r), :]
            ps[1, span(r + 1), :] = v.astype(BF16)
            sides(ps, r + 1, v)

        @pl.when(e == 1)
        def _():
            halo(2, ps, True)
            share_pass(1, ends_first)

    done, sent, plan = set(), [], []
    for i in (0, 2, 1):
        done.update((3 * i, 3 * i + 1, 3 * i + 2))
        ready = [y for y in ends_first if y not in sent and all(
            tap in done for tap in range(2 * y * sh // chans, (2 * (y + 1) * sh - 1) // chans + 1))]
        plan.append(ready)
        sent = sent + ready

    @pl.loop(0, taps)
    def _(e):
        @pl.when(e == 3)
        def _():
            share_start(0, plan[0])

        @pl.when(e == 6)
        def _():
            share_start(0, plan[1])
            share_pass(0, plan[0])

        i = (2 * (e // 3)) % 3
        j = e % 3
        put_grad(0, 3 * i + j, jnp.dot(x_t[:, span(i, rows)], ps[2 - j, span(1, rows), :],
                                       preferred_element_type=F32))

    share_start(0, plan[2])
    share_pass(0, plan[1])
    turn(0)
    share_pass(0, plan[2])

    @pl.loop(0, half)
    def _(e):
        @pl.when(e == half - 2)
        def _():
            halo(2, ps, False)
            edges(lambda r: sides(ps, r, ps[1, span(r), :].astype(F32)))
            share_finish(1)

        h = (2 * e + 2) % rows
        v = conv(ps, k_t.at[0], h, False) + ms[1, span(h + 1, 2), :].astype(F32)
        cot[span(h, 2), :] = v.astype(BF16)

    stores = [pltpu.make_async_copy(cot.at[pl.ds(r * cols, cols)], gi_hbm.at[r], loc_sem.at[r])
              for r in range(rows)]
    for cp in stores:
        cp.start()
    for cp in early:
        cp.wait_recv()
    share_finish(0)
    settle(1)
    settle(0)
    for cp in stores:
        cp.wait()
    for cp in started:
        cp.wait_send()
    for k in range(2):
        gather_close(k)
        share_close(k)
        for level in range(levels):
            gossip_copy(k, level).wait_send()


def copy_kernel(gi, nw, nm, gi_out, nw_out, nm_out, gi_at, w_at, m_at, came, left):
    rows = gi.shape[0]
    moves = [(gi.at[r], gi_at.at[r], gi_out.at[r]) for r in range(rows)]
    moves += [(nw.at[k], w_at.at[k], nw_out.at[k]) for k in range(2)]
    moves += [(nm.at[k], m_at.at[k], nm_out.at[k]) for k in range(2)]
    loads = [pltpu.make_async_copy(a, b, came.at[i]) for i, (a, b, _) in enumerate(moves)]
    stores = [pltpu.make_async_copy(b, d, left.at[i]) for i, (_, b, d) in enumerate(moves)]
    for cp in loads:
        cp.start()
    for a, b in zip(loads, stores):
        a.wait()
        b.start()
    for cp in stores:
        cp.wait()


def shards(inputs, cotangent, land_mask, weights, momentum, step):
    n = lax.axis_size("space")
    reps = lax.axis_size("replica")
    levels = reps.bit_length() - 1
    rows, cols, chans = inputs.shape[1:]
    sh = weights.shape[2]
    kc = sh * n
    ext = rows + 2
    nz = n // 2
    scale = 1.0 / math.sqrt(rows * n * cols)
    coef = (step[0] % levels == jnp.arange(levels)).astype(F32)
    vm = pltpu.VMEM
    sem = pltpu.SemaphoreType.DMA
    flops = 5 * 2 * rows * cols * kc * chans
    any_space = pl.BlockSpec(memory_space=pl.ANY)
    in_vmem = pl.BlockSpec(memory_space=pltpu.VMEM)
    gi, nw, nm = pl.pallas_call(
        partial(block_kernel, n, reps, levels, scale),
        out_shape=(
            jax.ShapeDtypeStruct((rows, cols, chans), BF16),
            jax.ShapeDtypeStruct((2, sh, chans), F32),
            jax.ShapeDtypeStruct((2, sh, chans), F32),
        ),
        in_specs=[pl.BlockSpec(memory_space=pltpu.SMEM), any_space, any_space,
                  in_vmem, in_vmem, in_vmem],
        out_specs=(any_space, in_vmem, in_vmem),
        scratch_shapes=[
            vm((3, ext * cols, chans), BF16),
            vm((3, ext * cols, chans), BF16),
            vm((3, ext * cols, chans), BF16),
            vm((chans, ext * cols), BF16),
            vm((chans, rows * cols), BF16),
            vm((rows * cols, chans), F32),
            vm((rows * cols, chans), BF16),
            vm((2, kc, chans), BF16),
            vm((2, kc, chans), BF16),
            vm((2, sh, chans), BF16),
            vm((2, sh, chans), BF16),
            vm((2, kc, chans), BF16),
            vm((2, nz, sh, chans), BF16),
            vm((2, nz, sh, chans), BF16),
            vm((2, nz, sh, chans), BF16),
            vm((2, sh, chans), BF16),
            vm((levels, 2, sh, chans), BF16),
            vm((levels, 2, sh, chans), BF16),
            vm((2, levels, sh, chans), BF16),
            sem((2 * rows,)),
            sem((3, 2)), sem((3, 2)),
            sem((2, 2, nz)), sem((2, 2, nz)), sem((2, 2, nz)), sem((2, 2, nz)),
            sem((2, nz)), sem((2, nz)), sem((2, nz)), sem((2, nz)),
            sem((4, levels)), sem((4, levels)),
        ],
        compiler_params=pltpu.CompilerParams(
            collective_id=0, has_side_effects=True, vmem_limit_bytes=63 * 1024 * 1024),
        cost_estimate=pl.CostEstimate(flops=flops, bytes_accessed=12 << 20, transcendentals=0),
    )(coef, inputs[0], cotangent[0], land_mask, weights[0], momentum[0])
    gi, nw, nm = pl.pallas_call(
        copy_kernel,
        out_shape=tuple(jax.ShapeDtypeStruct(v.shape, v.dtype) for v in (gi, nw, nm)),
        in_specs=[any_space] * 3,
        out_specs=(any_space,) * 3,
        scratch_shapes=[vm(gi.shape, BF16), vm(nw.shape, F32), vm(nm.shape, F32),
                        sem((rows + 4,)), sem((rows + 4,))],
        compiler_params=pltpu.CompilerParams(vmem_limit_bytes=63 * 1024 * 1024),
    )(gi, nw, nm)
    return gi[None], nw[None], nm[None]


def solution(mesh):
    in_specs = (
        P("replica", "space", None, None),
        P("replica", "space", None, None),
        P("space", None),
        P("replica", None, "space", None),
        P("replica", None, "space", None),
        P(),
    )
    out_specs = (
        P("replica", "space", None, None),
        P("replica", None, "space", None),
        P("replica", None, "space", None),
    )
    return jax.shard_map(shards, mesh=mesh, in_specs=in_specs, out_specs=out_specs, check_vma=False)
```
